32 devices in a mesh: dp: 32 (over z, y, x, core), tp: 1.
Axes of the slice: x: 2, y: 2, z: 4, core: 2. Of those that a mesh axis runs over, the one named last changes fastest.
Arguments:
- hidden: bfloat16 [1024, 4, 5120], P('dp', None, 'tp'), may hold values from -6 to 6
- norm_gain: bfloat16 [5120], P('tp'), may hold values from 0.3984375 to 2.5
- w_query: bfloat16 [5120, 4096], P(None, 'tp'), may hold values from -0.078125 to 0.078125
- key_projection: bfloat16 [5120, 1024], P(None, 'tp'), may hold values from -0.078125 to 0.078125
- value_projection: bfloat16 [5120, 1024], P(None, 'tp'), may hold values from -0.078125 to 0.078125
- query_gain: bfloat16 [128], replicated, may hold values from 0.5 to 2
- key_gain: bfloat16 [128], replicated, may hold values from 0.5 to 2
- cache_keys: bfloat16 [32, 32, 2, 128, 1024], P('dp', None, None, None, 'tp'), may hold values from -400 to 400
- cached_value_pages: bfloat16 [32, 32, 2, 128, 1024], P('dp', None, None, None, 'tp'), may hold values from -6 to 6
- cache_len: int32 [1024], replicated, may hold values from 1 to 256, as said below
- remaining: int32 [1024], P('dp'), may hold values from 0 to 7
- page_row: int32 [32, 32, 2], replicated, may hold values from 0 to 32, as said below
- page_seq: int32 [32, 32, 2], replicated, may hold values from 0 to 1, as said below
Outputs:
- attention: bfloat16 [1024, 4, 4096], P('dp', None, 'tp')
- new_keys: bfloat16 [1024, 4, 1024], P('dp', None, 'tp')
- new_values: bfloat16 [1024, 4, 1024], P('dp', None, 'tp')
The draws below stay inside these ranges and needn't reach their ends.
Inputs may be any that keep to these rules, and one draw needn't show every extreme that they name: `cache_len`: the pages of a row of n cached tokens fill exactly ceil(n / 128) slots. `page_row`: for holder group g, owner group o and slot c: the owner's row whose page the slot holds, or 32 for an empty slot. `page_seq`: each page number 0 to ceil(n / 128) - 1 of a row of n cached tokens appears once among the row's slots; empty slots hold 0.
All inputs are finite; a program needn't handle non-finite values.
Results may differ from the reference program's by a relative error of at most 0.015.
The reference program's roundings to bfloat16 on the way count: a program that leaves them out, or rounds other values in their place, can miss the bound.
Values may be sent and summed in bfloat16 or wider, within the bound.
A program may use at most 256 MiB of HBM per device.

```python
import math
import jax
import jax.numpy as jnp
from jax import lax

MODEL_WIDTH = 5120
HQ = 32
KEY_VALUE_HEADS = 8
HEAD_SIZE = 128
ROWS_DEV = 32
STEPS = 4
PAGE_TOKENS = 128
GROUP_ROW_SLOTS = 2
REPLICA_GROUPS = 32
ROWS = 1024
GROUP_SLOTS = 64
MAXP = 2


def group_state(base_key):
    state_key = jax.random.fold_in(base_key, 14)
    finished_groups = jax.random.randint(state_key, (REPLICA_GROUPS,), 0, 2)
    return finished_groups.at[0].set(0).at[1].set(1)


def page_layout(base_key):
    count_key = jax.random.fold_in(base_key, 11)
    tail_key = jax.random.fold_in(base_key, 12)
    shuffle_key = jax.random.fold_in(base_key, 13)
    counts = jax.random.randint(count_key, (REPLICA_GROUPS, ROWS_DEV), 1, MAXP + 1)
    counts = counts.at[0, 0].set(MAXP).at[0, 1].set(1)
    tails = jax.random.randint(tail_key, (REPLICA_GROUPS, ROWS_DEV), 1, PAGE_TOKENS + 1)
    tails = tails.at[0, 0].set(PAGE_TOKENS)
    return (counts, tails, shuffle_key)


def page_table(base_key):
    counts, tails, shuffle_key = page_layout(base_key)
    finished_groups = group_state(base_key)
    ends = jnp.cumsum(counts, axis=1)
    starts = ends - counts
    rank_position = jnp.arange(GROUP_SLOTS, dtype=jnp.int32)
    row_of = jnp.sum((rank_position[None, :, None] >= ends[:, None, :]).astype(jnp.int32), axis=2)
    safe_row = jnp.minimum(row_of, ROWS_DEV - 1)
    seq_of = jnp.where(row_of < ROWS_DEV, rank_position[None, :] - jnp.take_along_axis(starts, safe_row, axis=1), 0)
    random_jitter = jax.random.randint(shuffle_key, (REPLICA_GROUPS, GROUP_SLOTS), 0, 2 ** 20)
    holder_reward = finished_groups[rank_position // GROUP_ROW_SLOTS] * 2 ** 21
    group_scores = (random_jitter + holder_reward[None, :]) * GROUP_SLOTS + rank_position[None, :]
    placed = jnp.argsort(-group_scores, axis=1)
    inverse = jnp.argsort(placed, axis=1)
    row_slot = jnp.take_along_axis(row_of, inverse, axis=1)
    seq_slot = jnp.take_along_axis(seq_of, inverse, axis=1)
    row_table = row_slot.reshape(REPLICA_GROUPS, REPLICA_GROUPS, GROUP_ROW_SLOTS).transpose(1, 0, 2)
    seq_table = seq_slot.reshape(REPLICA_GROUPS, REPLICA_GROUPS, GROUP_ROW_SLOTS).transpose(1, 0, 2)
    return (row_table.astype(jnp.int32), seq_table.astype(jnp.int32))


def draw_cache_len(key, part):
    counts, tails, shuffle_key = page_layout(key)
    return ((counts - 1) * PAGE_TOKENS + tails).reshape(-1).astype(jnp.int32)


def draw_page_row(key, part):
    row_table, seq_table = page_table(key)
    return row_table


def draw_page_seq(key, part):
    row_table, seq_table = page_table(key)
    return seq_table


def draw_remaining(key, part):
    finished_groups = group_state(key)
    key = jax.random.fold_in(key, 4)
    busy_left = jax.random.randint(jax.random.fold_in(key, 1), (REPLICA_GROUPS, ROWS_DEV), 2, 8)
    done_left = jax.random.randint(jax.random.fold_in(key, 2), (REPLICA_GROUPS, ROWS_DEV), 0, 2)
    left = jnp.where(finished_groups[:, None] == 1, done_left, busy_left)
    left = left.at[0, 0].set(7).at[1, 0].set(0)
    return left.reshape(-1).astype(jnp.int32)


def draw_cache_keys(key, part):
    key = jax.random.fold_in(key, 5)
    base_offset = jax.random.normal(key, (REPLICA_GROUPS, REPLICA_GROUPS, GROUP_ROW_SLOTS, PAGE_TOKENS, KEY_VALUE_HEADS * HEAD_SIZE), jnp.float32)
    return jnp.clip(base_offset, -6.0, 6.0).astype(jnp.bfloat16)


def block_scale(own_key, extent, cuts, smallest, largest):
    loudness, own = 1.0, jax.random.fold_in(own_key, 6)
    for dim, shards_of in cuts:
        steps = jnp.exp(jax.random.uniform(jax.random.fold_in(own, dim), (shards_of,), jnp.float32, smallest / len(cuts), largest / len(cuts)))
        loudness = loudness * jnp.repeat(steps, extent[dim] // shards_of).reshape([-1 if axis == dim else 1 for axis in range(len(extent))])
    return loudness


def centred(rng, shape, spread, limit, shards=(), kind=jnp.bfloat16):
    entries = jax.random.normal(rng, shape, jnp.float32) * spread
    if len(shards) > 0:
        entries = block_scale(rng, shape, shards, -0.22, 0.18) * entries
    return jnp.clip(entries, min=-limit, max=limit).astype(kind)


def setup_inputs(seed: int = 0) -> dict:
    splits = jax.random.split(jax.random.key(seed), 14)
    hidden = centred(splits[0], (ROWS, STEPS, MODEL_WIDTH), 1.0, 6.0, ((0, 32),))
    norm_gain = jnp.clip(jnp.exp(jax.random.uniform(splits[1], (MODEL_WIDTH,), jnp.float32, math.log(0.3984375), math.log(2.5))), 0.3984375, 2.5).astype(jnp.bfloat16)
    w_query = centred(splits[2], (MODEL_WIDTH, HQ * HEAD_SIZE), MODEL_WIDTH ** -0.5, 0.078125)
    key_projection = centred(splits[3], (MODEL_WIDTH, KEY_VALUE_HEADS * HEAD_SIZE), MODEL_WIDTH ** -0.5, 0.078125)
    value_projection = centred(splits[4], (MODEL_WIDTH, KEY_VALUE_HEADS * HEAD_SIZE), MODEL_WIDTH ** -0.5, 0.078125)
    query_gain = jnp.clip(jnp.exp(jax.random.uniform(splits[5], (HEAD_SIZE,), jnp.float32, math.log(0.5), math.log(2.0))), 0.5, 2.0).astype(jnp.bfloat16)
    key_gain = jnp.clip(jnp.exp(jax.random.uniform(splits[6], (HEAD_SIZE,), jnp.float32, math.log(0.5), math.log(2.0))), 0.5, 2.0).astype(jnp.bfloat16)
    cache_keys = draw_cache_keys(jax.random.fold_in(splits[13], 71), 0)
    cached_value_pages = centred(splits[8], (REPLICA_GROUPS, REPLICA_GROUPS, GROUP_ROW_SLOTS, PAGE_TOKENS, KEY_VALUE_HEADS * HEAD_SIZE), 1.0, 6.0, ((0, 32),))
    cache_len = draw_cache_len(jax.random.fold_in(splits[13], 71), 0)
    remaining = draw_remaining(jax.random.fold_in(splits[13], 71), 0)
    page_row = draw_page_row(jax.random.fold_in(splits[13], 71), 0)
    page_seq = draw_page_seq(jax.random.fold_in(splits[13], 71), 0)
    return {"hidden": hidden, "norm_gain": norm_gain, "w_query": w_query, "key_projection": key_projection, "value_projection": value_projection, "query_gain": query_gain, "key_gain": key_gain, "cache_keys": cache_keys, "cached_value_pages": cached_value_pages, "cache_len": cache_len, "remaining": remaining, "page_row": page_row, "page_seq": page_seq}


EPSILON = 1e-06
ROPE_BASE = 1000000.0
MASKED_SCORE = -1e+30

def head_norm_rope(heads, gain_vector, positions):
    head_width = heads.shape[-1]
    half_width = head_width // 2
    scaled = heads * lax.rsqrt(lax.optimization_barrier(jnp.mean(heads * heads, axis=-1, keepdims=True)) + EPSILON) * gain_vector.astype(jnp.float32)
    frequency = jnp.exp(jnp.arange(half_width, dtype=jnp.float32) * (-2.0 * math.log(ROPE_BASE) / head_width))
    angles = positions.astype(jnp.float32)[:, :, None, None] * frequency
    cosine = jnp.cos(angles)
    sine_part = jnp.sin(angles)
    first_half = scaled[..., :half_width]
    second = scaled[..., half_width:]
    return jnp.concatenate([first_half * cosine - second * sine_part, second * cosine + first_half * sine_part], axis=-1)

def masked_parts(group_scores, usable):
    group_scores = jnp.where(usable, group_scores, MASKED_SCORE)
    block_max = lax.optimization_barrier(jnp.max(group_scores, axis=-1))
    weights = jnp.where(usable, jnp.exp(group_scores - block_max[..., None]), 0.0).astype(jnp.bfloat16)
    return (block_max, weights, lax.optimization_barrier(jnp.sum(weights.astype(jnp.float32), axis=-1)))

def page_partial(queries, page_keys, page_values, usable):
    scale = 1.0 / math.sqrt(queries.shape[-1])
    group_scores = jnp.einsum('nkqd,npkd->nkqp', queries.astype(jnp.float32), page_keys.astype(jnp.float32)) * scale
    block_max, weights, block_total = masked_parts(group_scores, usable[:, None, None, :])
    output = jnp.einsum('nkqp,npkd->nkqd', weights.astype(jnp.float32), page_values.astype(jnp.float32))
    return (block_max, block_total, output)

def new_partial(arranged, fresh_keys, fresh_values, step_count):
    scale = 1.0 / math.sqrt(arranged.shape[-1])
    group_scores = jnp.einsum('rkqd,rjkd->rkqj', arranged.astype(jnp.float32), fresh_keys.astype(jnp.float32)) * scale
    step_index = jnp.arange(arranged.shape[2], dtype=jnp.int32) % step_count
    causal = jnp.arange(step_count, dtype=jnp.int32)[None, :] <= step_index[:, None]
    block_max, weights, block_total = masked_parts(group_scores, causal[None, None])
    output = jnp.einsum('rkqj,rjkd->rkqd', weights.astype(jnp.float32), fresh_values.astype(jnp.float32))
    return (block_max, block_total, output)

def combine_pages(page_rows, page_max, page_total, page_out, new_max, new_total, new_out, row_count):
    row_hit = (page_rows[:, None] == jnp.arange(row_count, dtype=jnp.int32)[None, :])[:, :, None, None]
    page_top = lax.optimization_barrier(jnp.max(jnp.where(row_hit, page_max[:, None], MASKED_SCORE), axis=0))
    row_max = jnp.maximum(page_top, new_max)
    factor = jnp.exp(jnp.where(row_hit, page_max[:, None] - row_max[None], MASKED_SCORE))
    own_factor = jnp.exp(new_max - row_max)
    denominator = jnp.einsum('nrkq,nkq->rkq', factor, page_total, precision=lax.Precision.HIGHEST) + own_factor * new_total
    numerator = jnp.einsum('nrkq,nkqd->rkqd', factor, page_out, precision=lax.Precision.HIGHEST) + own_factor[..., None] * new_out
    return numerator / denominator[..., None]

def reference(hidden, norm_gain, w_query, key_projection, value_projection, query_gain, key_gain, cache_keys, cached_value_pages, cache_len, remaining, page_row, page_seq):
    row_count, step_count, feature_count = hidden.shape
    head_width = query_gain.shape[0]
    groups = page_row.shape[0]
    per_group = row_count // groups
    page_len = cache_keys.shape[3]
    hidden_wide = hidden.astype(jnp.float32)
    normed = (hidden_wide * lax.rsqrt(lax.optimization_barrier(jnp.mean(hidden_wide * hidden_wide, axis=-1, keepdims=True)) + EPSILON) * norm_gain.astype(jnp.float32)).astype(jnp.bfloat16)
    flattened = normed.reshape(row_count * step_count, feature_count)
    positions = cache_len[:, None] + jnp.arange(step_count, dtype=jnp.int32)[None, :]
    queries = jnp.dot(flattened, w_query, preferred_element_type=jnp.float32).reshape(row_count, step_count, -1, head_width)
    queries = head_norm_rope(queries, query_gain, positions).astype(jnp.bfloat16)
    fresh_keys = jnp.dot(flattened, key_projection, preferred_element_type=jnp.float32).reshape(row_count, step_count, -1, head_width)
    fresh_keys = head_norm_rope(fresh_keys, key_gain, positions).astype(jnp.bfloat16)
    fresh_values = jnp.dot(flattened, value_projection, preferred_element_type=jnp.float32).astype(jnp.bfloat16).reshape(row_count, step_count, -1, head_width)
    kv_heads = fresh_keys.shape[2]
    group_size = queries.shape[2] // kv_heads
    arranged = queries.reshape(row_count, step_count, kv_heads, group_size, head_width).transpose(0, 2, 3, 1, 4).reshape(row_count, kv_heads, group_size * step_count, head_width)
    new_max, new_total, new_out = new_partial(arranged, fresh_keys, fresh_values, step_count)

    def one_owner(owner_group):
        row_start = owner_group * per_group
        owner_queries = lax.dynamic_slice_in_dim(arranged, row_start, per_group, 0)
        owner_lengths = lax.dynamic_slice_in_dim(cache_len, row_start, per_group, 0)
        page_keys = lax.dynamic_index_in_dim(cache_keys, owner_group, 1, keepdims=False).reshape(-1, page_len, kv_heads, head_width)
        page_values = lax.dynamic_index_in_dim(cached_value_pages, owner_group, 1, keepdims=False).reshape(-1, page_len, kv_heads, head_width)
        page_rows = lax.dynamic_index_in_dim(page_row, owner_group, 1, keepdims=False).reshape(-1)
        page_numbers = lax.dynamic_index_in_dim(page_seq, owner_group, 1, keepdims=False).reshape(-1)
        safe_row = jnp.minimum(page_rows, per_group - 1)
        length_cap = jnp.where(page_rows < per_group, owner_lengths[safe_row], 0)
        usable = page_numbers[:, None] * page_len + jnp.arange(page_len, dtype=jnp.int32)[None, :] < length_cap[:, None]
        page_max, page_total, page_out = page_partial(owner_queries[safe_row], page_keys, page_values, usable)
        return combine_pages(page_rows, page_max, page_total, page_out, lax.dynamic_slice_in_dim(new_max, row_start, per_group, 0), lax.dynamic_slice_in_dim(new_total, row_start, per_group, 0), lax.dynamic_slice_in_dim(new_out, row_start, per_group, 0), per_group)
    attended = lax.map(one_owner, jnp.arange(groups, dtype=jnp.int32)).reshape(row_count, kv_heads, group_size, step_count, head_width)
    attended = attended.transpose(0, 3, 1, 2, 4).reshape(row_count, step_count, -1)
    live = jnp.arange(step_count, dtype=jnp.int32)[None, :] < remaining[:, None]
    attention = jnp.where(live[:, :, None], attended, 0.0).astype(jnp.bfloat16)
    return (attention, fresh_keys.reshape(row_count, step_count, -1), fresh_values.reshape(row_count, step_count, -1))
```

```python
import functools
import math

import jax
import jax.numpy as jnp
from jax import lax
from jax.experimental import pallas as pl
from jax.experimental.pallas import tpu as pltpu
from jax.sharding import PartitionSpec as P

EPSILON = 1e-06
ROPE_BASE = 1000000.0
MASKED_SCORE = -1e30
DEPTH = 4
WEIGHT_BUFFERS = 3


def soft_parts(scores, mask, head_width):
    scores = jnp.where(mask, scores * (1.0 / math.sqrt(head_width)), MASKED_SCORE)
    top = jnp.max(scores, axis=0, keepdims=True)
    weights = jnp.where(mask, jnp.exp(scores - top), 0.0)
    weights = weights.astype(jnp.bfloat16).astype(jnp.float32)
    return top, jnp.sum(weights, axis=0, keepdims=True), weights.T.astype(jnp.bfloat16)


def spread_dot(keys, block_q):
    return lax.dot_general(
        keys, block_q, (((1,), (1,)), ((), ())), preferred_element_type=jnp.float32
    )


def exchange_kernel(
    n,
    sizes,
    row_ref,
    seq_ref,
    len_ref,
    slot_ref,
    x_ref,
    gain_ref,
    cos_ref,
    sin_ref,
    q_gain_ref,
    k_gain_ref,
    wq_ref,
    wk_ref,
    wv_ref,
    ck_ref,
    cv_ref,
    out_ref,
    nk_ref,
    nv_ref,
    normed,
    wbuf,
    q_own,
    q_send,
    q_recv,
    o_send,
    o_recv,
    s_send,
    s_recv,
    kbuf,
    vbuf,
    block_q,
    new_o,
    new_s,
    q_ssem,
    q_rsem,
    o_ssem,
    o_rsem,
    s_ssem,
    s_rsem,
    ksem,
    vsem,
    wsem,
):
    rows, heads, per_head, head_width, steps, cap, page, depth, parts = sizes
    width = heads * per_head
    part_heads = heads // parts
    part_rows = part_heads * per_head
    block_cols = wbuf.shape[2]
    key_cols = min(block_cols, wk_ref.shape[1])
    key_blocks = wk_ref.shape[1] // key_cols
    blocks = heads + 2 * key_blocks
    bufs = wbuf.shape[0]
    me = lax.axis_index("dp")

    def distance(k):
        return k // 2 + (n // 2) * lax.rem(k, 2)

    def after(k):
        return lax.rem(me + distance(k), n)

    def before(k):
        return lax.rem(me + n - distance(k), n)

    def own_row(holder, c):
        return jnp.minimum(row_ref[(holder * n + me) * cap + c], rows - 1)

    def usable_tokens(owner, c):
        index = (me * n + owner) * cap + c
        row = row_ref[index]
        length = len_ref[owner * rows + jnp.minimum(row, rows - 1)]
        return jnp.where(row < rows, length, 0) - seq_ref[index] * page

    def fetch(k):
        owner, buf = before(k), lax.rem(k, depth)
        return (
            pltpu.make_async_copy(ck_ref.at[owner], kbuf.at[buf], ksem.at[buf]),
            pltpu.make_async_copy(cv_ref.at[owner], vbuf.at[buf], vsem.at[buf]),
        )

    def weight(j, act):
        buf = lax.rem(j, bufs)

        def move(ref, at, cols):
            src = ref.at[:, pl.ds(pl.multiple_of(at * cols, cols), cols)]
            dst = wbuf.at[buf, :, pl.ds(0, cols)]
            act(pltpu.make_async_copy(src, dst, wsem.at[buf]))

        @pl.when(j < heads)
        def _():
            move(wq_ref, j, block_cols)

        @pl.when((j >= heads) & (j < heads + key_blocks))
        def _():
            move(wk_ref, j - heads, key_cols)

        @pl.when((j >= heads + key_blocks) & (j < blocks))
        def _():
            move(wv_ref, j - heads - key_blocks, key_cols)

    def start(copy):
        copy.start()

    def wait(copy):
        copy.wait()

    def project(j, cols):
        weight(j + bufs - 1, start)
        weight(j, wait)
        return jnp.dot(
            normed[...],
            wbuf[lax.rem(j, bufs), :, 0:cols],
            preferred_element_type=jnp.float32,
        )

    def rotated(made, gain):
        done = []
        for h in range(made.shape[1] // head_width):
            y = made[:, h * head_width : (h + 1) * head_width]
            y = y * lax.rsqrt(jnp.mean(y * y, axis=-1, keepdims=True) + EPSILON) * gain
            done.append(y * cos_ref[...] + pltpu.roll(y, head_width // 2, 1) * sin_ref[...])
        return done

    def send_query(part, k):
        peer = after(k)
        return pltpu.make_async_remote_copy(
            src_ref=q_send.at[part, peer],
            dst_ref=q_recv.at[part, me],
            send_sem=q_ssem.at[part, peer],
            recv_sem=q_rsem.at[part, me],
            device_id={"dp": peer},
            device_id_type=pl.DeviceIdType.MESH,
        )

    def recv_query(part, k):
        owner = before(k)
        return pltpu.make_async_remote_copy(
            src_ref=q_send.at[part, owner],
            dst_ref=q_recv.at[part, owner],
            send_sem=q_ssem.at[part, owner],
            recv_sem=q_rsem.at[part, owner],
            device_id={"dp": owner},
            device_id_type=pl.DeviceIdType.MESH,
        )

    def send_back(owner, slot):
        to = dict(device_id={"dp": owner}, device_id_type=pl.DeviceIdType.MESH)
        return (
            pltpu.make_async_remote_copy(
                src_ref=o_send.at[owner],
                dst_ref=o_recv.at[slot],
                send_sem=o_ssem.at[owner],
                recv_sem=o_rsem.at[slot],
                **to,
            ),
            pltpu.make_async_remote_copy(
                src_ref=s_send.at[owner],
                dst_ref=s_recv.at[slot],
                send_sem=s_ssem.at[owner],
                recv_sem=s_rsem.at[slot],
                **to,
            ),
        )

    for j in range(bufs - 1):
        weight(jnp.int32(j), start)
    for k in range(depth - 1):
        for copy in fetch(k):
            copy.start()

    barrier = pltpu.get_barrier_semaphore()

    @pl.loop(1, n)
    def _(k):
        pl.semaphore_signal(
            barrier, inc=1, device_id={"dp": after(k)}, device_id_type=pl.DeviceIdType.MESH
        )

    block_q[...] = jnp.zeros_like(block_q)
    x = x_ref[...].astype(jnp.float32).reshape(normed.shape)
    scale = lax.rsqrt(jnp.mean(x * x, axis=-1, keepdims=True) + EPSILON)
    normed[...] = (x * scale * gain_ref[...].astype(jnp.float32)).astype(jnp.bfloat16)

    for part in range(parts):

        @pl.loop(part * part_heads, (part + 1) * part_heads)
        def _(h):
            done = rotated(project(h, block_cols), q_gain_ref[...].astype(jnp.float32))
            done = [y.reshape(rows, steps, head_width) for y in done]
            at = pl.ds(pl.multiple_of(h * per_head, per_head), per_head)
            q_own[:, at, :] = jnp.concatenate(done, axis=1).astype(jnp.bfloat16)

        if part == 0:
            pl.semaphore_wait(barrier, n - 1)
        span = slice(part * part_rows, (part + 1) * part_rows)

        @pl.loop(1, n)
        def _(k):
            peer = after(k)
            for c in range(cap):
                q_send[part, peer, c] = q_own[own_row(peer, c), span]
            send_query(part, k).start()

        for c in range(cap):
            q_recv[part, me, c] = q_own[own_row(me, c), span]

    @pl.loop(0, key_blocks)
    def _(j):
        done = rotated(project(j + heads, key_cols), k_gain_ref[...].astype(jnp.float32))
        at = pl.ds(pl.multiple_of(j * key_cols, key_cols), key_cols)
        nk_ref[:, at] = jnp.concatenate(done, axis=1).astype(jnp.bfloat16)

    @pl.loop(0, key_blocks)
    def _(j):
        at = pl.ds(pl.multiple_of(j * key_cols, key_cols), key_cols)
        nv_ref[:, at] = project(j + heads + key_blocks, key_cols).astype(jnp.bfloat16)

    position = lax.broadcasted_iota(jnp.int32, (page, width), 0)

    def columns(h):
        return slice(h * head_width, (h + 1) * head_width)

    def stripe(h):
        return slice(h * per_head, (h + 1) * per_head)

    @pl.loop(0, n)
    def _(k):
        owner, buf = before(k), lax.rem(k, depth)

        @pl.when(k + depth - 1 < n)
        def _():
            for copy in fetch(k + depth - 1):
                copy.start()

        @pl.when(k > 0)
        def _():
            for part in range(parts):
                recv_query(part, k).wait_recv()

        for copy in fetch(k):
            copy.wait()
        scores = []
        for c in range(cap):
            for h in range(heads):
                part, first = h // part_heads, (h % part_heads) * per_head
                block_q[c, stripe(h), columns(h)] = q_recv[
                    part, owner, c, first : first + per_head
                ]
            scores.append(spread_dot(kbuf[buf, c], block_q[c]))
        turned = []
        for c in range(cap):
            mask = position < usable_tokens(owner, c)
            top, total, weights = soft_parts(scores[c], mask, head_width)
            s_send[owner, 2 * c : 2 * c + 1, 0:width] = top
            s_send[owner, 2 * c + 1 : 2 * c + 2, 0:width] = total
            turned.append(weights)
        for c in range(cap):
            for h in range(heads):
                o_send[owner, c, stripe(h)] = jnp.dot(
                    turned[c][stripe(h)],
                    vbuf[buf, c, :, columns(h)],
                    preferred_element_type=jnp.float32,
                ).astype(jnp.bfloat16)

        @pl.when(k > 0)
        def _():
            for copy in send_back(owner, me):
                copy.start()

    per_tile = 16 // steps
    token = lax.broadcasted_iota(jnp.int32, (16, width), 0)
    step = lax.rem(lax.broadcasted_iota(jnp.int32, (16, width), 1), steps)
    masks = [(token >= i * steps) & (token <= i * steps + step) for i in range(per_tile)]

    @pl.loop(0, rows // per_tile)
    def _(tile):
        at = pl.ds(pl.multiple_of(tile * 16, 16), 16)
        keys, values = nk_ref[at], nv_ref[at]
        scores = []
        for i in range(per_tile):
            for h in range(heads):
                block_q[i, stripe(h), columns(h)] = q_own[tile * per_tile + i, stripe(h)]
            scores.append(spread_dot(keys, block_q[i]))
        turned = []
        for i in range(per_tile):
            row = tile * per_tile + i
            top, total, weights = soft_parts(scores[i], masks[i], head_width)
            new_s[row, 0:1, 0:width] = top
            new_s[row, 1:2, 0:width] = total
            turned.append(weights)
        for h in range(heads):
            stacked = jnp.concatenate([w[stripe(h)] for w in turned], axis=0)
            outs = jnp.dot(stacked, values[:, columns(h)], preferred_element_type=jnp.float32)
            for i in range(per_tile):
                new_o[tile * per_tile + i, stripe(h)] = outs[stripe(i)]

    o_recv[me] = o_send[me]
    s_recv[me] = s_send[me]

    @pl.loop(1, n)
    def _(k):
        for part in range(parts):
            send_query(part, k).wait_send()
        for copy in send_back(before(k), me):
            copy.wait_send()
        for copy in send_back(after(k), after(k)):
            copy.wait_recv()

    @pl.loop(0, rows, unroll=2)
    def _(r):
        first, second = slot_ref[r], slot_ref[rows + r]
        has_second = slot_ref[2 * rows + r]

        def stats(slot):
            both = s_recv[slot // cap]
            top, total = both[0:1], both[1:2]
            for c in range(1, cap):
                hit = lax.rem(slot, cap) == c
                top = jnp.where(hit, both[2 * c : 2 * c + 1], top)
                total = jnp.where(hit, both[2 * c + 1 : 2 * c + 2], total)
            return top, total

        top_a, total_a = stats(first)
        top_b, total_b = stats(second)
        top_b = jnp.where(has_second > 0, top_b, MASKED_SCORE)
        total_b = jnp.where(has_second > 0, total_b, 0.0)
        top_n, total_n = new_s[r, 0:1], new_s[r, 1:2]
        top = jnp.maximum(jnp.maximum(top_a, top_b), top_n)
        fa, fb, fn = jnp.exp(top_a - top), jnp.exp(top_b - top), jnp.exp(top_n - top)
        fb = jnp.where(has_second > 0, fb, 0.0)
        share = 1.0 / (fa * total_a + fb * total_b + fn * total_n)
        factors = jnp.concatenate(
            [fa * share, fb * share, fn * share, jnp.zeros((5, fa.shape[1]), jnp.float32)], axis=0
        ).T[0:width]
        out_a = o_recv[first // cap, lax.rem(first, cap)].astype(jnp.float32)
        out_b = o_recv[second // cap, lax.rem(second, cap)].astype(jnp.float32)
        out = factors[:, 0:1] * out_a + factors[:, 1:2] * out_b + factors[:, 2:3] * new_o[r]
        out_ref[r] = out.astype(out_ref.dtype)


def shards(
    hidden,
    norm_gain,
    w_query,
    key_projection,
    value_projection,
    query_gain,
    key_gain,
    cache_keys,
    cached_value_pages,
    cache_len,
    remaining,
    page_row,
    page_seq,
):
    gathered, full_gain = (
        lax.all_gather(hidden, "tp", axis=2, tiled=True),
        lax.all_gather(norm_gain, "tp", axis=0, tiled=True),
    )
    row_count, step_count, feature_count = gathered.shape
    head_width = query_gain.shape[0]
    groups = page_row.shape[0]
    capacity = page_row.shape[2]
    page_len = cache_keys.shape[3]
    kv_heads = key_projection.shape[1] // head_width
    my_group = lax.axis_index("dp")
    tokens = row_count * step_count
    local_lengths = lax.dynamic_slice_in_dim(cache_len, my_group * row_count, row_count)
    positions = local_lengths[:, None] + jnp.arange(step_count, dtype=jnp.int32)[None, :]
    half = head_width // 2
    frequency = jnp.exp(
        jnp.arange(half, dtype=jnp.float32) * (-2.0 * math.log(ROPE_BASE) / head_width)
    )
    angles = positions.astype(jnp.float32).reshape(tokens, 1) * frequency
    cosine, sine = jnp.cos(angles), jnp.sin(angles)
    cosine = jnp.concatenate([cosine, cosine], axis=1)
    sine = jnp.concatenate([-sine, sine], axis=1)
    query_heads = w_query.shape[1] // head_width
    group_size = query_heads // kv_heads
    per_head = group_size * step_count
    sent_rows = lax.dynamic_index_in_dim(page_row, my_group, 1, keepdims=False).reshape(-1)
    sent_seq = lax.dynamic_index_in_dim(page_seq, my_group, 1, keepdims=False).reshape(-1)
    row_index = jnp.arange(row_count, dtype=jnp.int32)[:, None]
    holds = sent_rows[None, :] == row_index
    slot_count = groups * capacity
    slot_index = jnp.arange(slot_count, dtype=jnp.int32)[None, :]
    shifted = slot_index * jnp.where(sent_seq == 0, 1, slot_count)[None, :]
    both = jnp.sum(jnp.where(holds, shifted, 0), axis=1)
    slot_a, slot_b = both % slot_count, both // slot_count
    has_b = (local_lengths > page_len).astype(jnp.int32)
    slots = jnp.concatenate([slot_a, slot_b, has_b])
    width = kv_heads * per_head
    lanes = max(128, width)
    sizes = (row_count, kv_heads, per_head, head_width, step_count, capacity, page_len)
    parts = 2 if kv_heads % 2 == 0 else 1
    sizes = sizes + (DEPTH, parts)
    smem = pl.BlockSpec(memory_space=pltpu.SMEM)
    vmem = pl.BlockSpec(memory_space=pltpu.VMEM)
    hbm = pl.BlockSpec(memory_space=pl.ANY)
    bf16, f32 = jnp.bfloat16, jnp.float32
    features = kv_heads * head_width
    dma = pltpu.SemaphoreType.DMA
    attended, fresh_keys, fresh_values = pl.pallas_call(
        functools.partial(exchange_kernel, groups, sizes),
        out_shape=(
            jax.ShapeDtypeStruct((row_count, width, head_width), bf16),
            jax.ShapeDtypeStruct((tokens, features), bf16),
            jax.ShapeDtypeStruct((tokens, features), bf16),
        ),
        in_specs=[smem] * 4 + [vmem] * 6 + [hbm] * 5,
        out_specs=(vmem, vmem, vmem),
        scratch_shapes=[
            pltpu.VMEM((tokens, feature_count), bf16),
            pltpu.VMEM((WEIGHT_BUFFERS, feature_count, group_size * head_width), bf16),
            pltpu.VMEM((row_count, width, head_width), bf16),
            pltpu.VMEM((parts, groups, capacity, width // parts, head_width), bf16),
            pltpu.VMEM((parts, groups, capacity, width // parts, head_width), bf16),
            pltpu.VMEM((groups, capacity, width, head_width), bf16),
            pltpu.VMEM((groups, capacity, width, head_width), bf16),
            pltpu.VMEM((groups, 2 * capacity, lanes), f32),
            pltpu.VMEM((groups, 2 * capacity, lanes), f32),
            pltpu.VMEM((DEPTH, capacity, page_len, features), bf16),
            pltpu.VMEM((DEPTH, capacity, page_len, features), bf16),
            pltpu.VMEM((max(capacity, 16 // step_count), width, features), bf16),
            pltpu.VMEM((row_count, width, head_width), f32),
            pltpu.VMEM((row_count, 2, lanes), f32),
        ]
        + [dma((parts, groups))] * 2
        + [dma((groups,))] * 4
        + [dma((DEPTH,))] * 2
        + [dma((WEIGHT_BUFFERS,))],
        compiler_params=pltpu.CompilerParams(
            collective_id=0, has_side_effects=True, vmem_limit_bytes=56 * 1024 * 1024
        ),
        name="page_exchange",
    )(
        page_row.reshape(-1),
        page_seq.reshape(-1),
        cache_len,
        slots,
        gathered,
        full_gain.reshape(1, feature_count),
        cosine,
        sine,
        query_gain.reshape(1, head_width),
        key_gain.reshape(1, head_width),
        w_query,
        key_projection,
        value_projection,
        cache_keys.reshape(groups, capacity, page_len, features),
        cached_value_pages.reshape(groups, capacity, page_len, features),
    )
    attended = (
        attended.reshape(row_count, kv_heads, group_size, step_count, head_width)
        .transpose(0, 3, 1, 2, 4)
        .reshape(row_count, step_count, -1)
    )
    live = jnp.arange(step_count, dtype=jnp.int32)[None, :] < remaining[:, None]
    attention = jnp.where(live[:, :, None], attended, 0.0).astype(jnp.bfloat16)
    return (
        attention,
        fresh_keys.reshape(row_count, step_count, -1),
        fresh_values.reshape(row_count, step_count, -1),
    )


def solution(mesh):
    in_specs = (
        P("dp", None, "tp"),
        P("tp"),
        P(None, "tp"),
        P(None, "tp"),
        P(None, "tp"),
        P(),
        P(),
        P("dp", None, None, None, "tp"),
        P("dp", None, None, None, "tp"),
        P(),
        P("dp"),
        P(),
        P(),
    )
    out_specs = (P("dp", None, "tp"), P("dp", None, "tp"), P("dp", None, "tp"))
    return jax.shard_map(shards, mesh=mesh, in_specs=in_specs, out_specs=out_specs, check_vma=False)
```

```python
import functools
import math

import jax
import jax.numpy as jnp
from jax import lax
from jax.experimental import pallas as pl
from jax.experimental.pallas import tpu as pltpu
from jax.sharding import PartitionSpec as P

EPSILON = 1e-06
ROPE_BASE = 1000000.0
MASKED_SCORE = -1e30
DEPTH = 6
PAIR = 2
WEIGHT_BUFFERS = 3


def soft_parts(scores, mask, head_width):
    scores = jnp.where(mask, scores * (1.0 / math.sqrt(head_width)), MASKED_SCORE)
    top = jnp.maximum(jnp.max(scores, axis=0, keepdims=True), 0.1 * MASKED_SCORE)
    weights = jnp.exp(scores - top).astype(jnp.bfloat16).astype(jnp.float32)
    return top, jnp.sum(weights, axis=0, keepdims=True), weights.T.astype(jnp.bfloat16)


def spread_dot(keys, queries, heads, per_head):
    turned = queries.astype(jnp.float32).T.astype(jnp.bfloat16)
    head_of = lax.broadcasted_iota(jnp.int32, turned.shape, 1) // per_head
    spread = [jnp.where(head_of == h, turned, jnp.zeros_like(turned)) for h in range(heads)]
    return jnp.dot(
        keys, jnp.concatenate(spread, axis=0), preferred_element_type=jnp.float32
    )


def exchange_kernel(
    n,
    sizes,
    table_ref,
    len_ref,
    x_ref,
    gain_ref,
    cos_ref,
    sin_ref,
    q_gain_ref,
    k_gain_ref,
    wq_ref,
    wk_ref,
    wv_ref,
    ck_ref,
    cv_ref,
    out_ref,
    nk_ref,
    nv_ref,
    normed,
    wbuf,
    q_own,
    q_send,
    q_recv,
    o_send,
    o_recv,
    s_send,
    s_recv,
    kbuf,
    vbuf,
    new_o,
    new_s,
    q_ssem,
    q_rsem,
    o_ssem,
    o_rsem,
    s_ssem,
    s_rsem,
    ksem,
    vsem,
    wsem,
):
    rows, heads, per_head, head_width, steps, cap, page, depth, parts = sizes
    width = heads * per_head
    part_heads = heads // parts
    part_rows = part_heads * per_head
    block_cols = wbuf.shape[2]
    key_cols = min(block_cols, wk_ref.shape[1])
    key_blocks = wk_ref.shape[1] // key_cols
    blocks = heads + 2 * key_blocks
    bufs = wbuf.shape[0]
    me = lax.axis_index("dp")

    def distance(k):
        return k // 2 + (n // 2) * lax.rem(k, 2)

    def after(k):
        return lax.rem(me + distance(k), n)

    def before(k):
        return lax.rem(me + n - distance(k), n)

    count = n * cap

    def own_row(holder, c):
        return table_ref[holder * cap + c]

    def usable_tokens(owner, c):
        index = count + owner * cap + c
        row = table_ref[index]
        length = len_ref[owner * rows + jnp.minimum(row, rows - 1)]
        return jnp.where(row < rows, length, 0) - table_ref[index + count] * page

    def fetch(k):
        owner, buf = before(k), lax.rem(k, depth)
        return (
            pltpu.make_async_copy(ck_ref.at[owner], kbuf.at[buf], ksem.at[buf]),
            pltpu.make_async_copy(cv_ref.at[owner], vbuf.at[buf], vsem.at[buf]),
        )

    def weight(j, act):
        buf = lax.rem(j, bufs)

        def move(ref, at, cols):
            src = ref.at[:, pl.ds(pl.multiple_of(at * cols, cols), cols)]
            dst = wbuf.at[buf, :, pl.ds(0, cols)]
            act(pltpu.make_async_copy(src, dst, wsem.at[buf]))

        @pl.when(j < heads)
        def _():
            move(wq_ref, j, block_cols)

        @pl.when((j >= heads) & (j < heads + key_blocks))
        def _():
            move(wk_ref, j - heads, key_cols)

        @pl.when((j >= heads + key_blocks) & (j < blocks))
        def _():
            move(wv_ref, j - heads - key_blocks, key_cols)

    def start(copy):
        copy.start()

    def wait(copy):
        copy.wait()

    def project(j, cols):
        weight(j + bufs - 1, start)
        weight(j, wait)
        return jnp.dot(
            normed[...],
            wbuf[lax.rem(j, bufs), :, 0:cols],
            preferred_element_type=jnp.float32,
        )

    def rotated(made, gain):
        done = []
        for h in range(made.shape[1] // head_width):
            y = made[:, h * head_width : (h + 1) * head_width]
            y = y * lax.rsqrt(jnp.mean(y * y, axis=-1, keepdims=True) + EPSILON) * gain
            done.append(y * cos_ref[...] + pltpu.roll(y, head_width // 2, 1) * sin_ref[...])
        return done

    def send_query(part, k):
        peer = after(k)
        return pltpu.make_async_remote_copy(
            src_ref=q_send.at[part, peer],
            dst_ref=q_recv.at[part, me],
            send_sem=q_ssem.at[part, peer],
            recv_sem=q_rsem.at[part, me],
            device_id={"dp": peer},
            device_id_type=pl.DeviceIdType.MESH,
        )

    def recv_query(part, k):
        owner = before(k)
        return pltpu.make_async_remote_copy(
            src_ref=q_send.at[part, owner],
            dst_ref=q_recv.at[part, owner],
            send_sem=q_ssem.at[part, owner],
            recv_sem=q_rsem.at[part, owner],
            device_id={"dp": owner},
            device_id_type=pl.DeviceIdType.MESH,
        )

    def send_back(owner, slot):
        to = dict(device_id={"dp": owner}, device_id_type=pl.DeviceIdType.MESH)
        return (
            pltpu.make_async_remote_copy(
                src_ref=o_send.at[owner],
                dst_ref=o_recv.at[slot],
                send_sem=o_ssem.at[owner],
                recv_sem=o_rsem.at[slot],
                **to,
            ),
            pltpu.make_async_remote_copy(
                src_ref=s_send.at[owner],
                dst_ref=s_recv.at[slot],
                send_sem=s_ssem.at[owner],
                recv_sem=s_rsem.at[slot],
                **to,
            ),
        )

    for j in range(bufs - 1):
        weight(jnp.int32(j), start)
    for k in range(depth - PAIR):
        for copy in fetch(k):
            copy.start()

    barrier = pltpu.get_barrier_semaphore()

    @pl.loop(1, n)
    def _(k):
        pl.semaphore_signal(
            barrier, inc=1, device_id={"dp": after(k)}, device_id_type=pl.DeviceIdType.MESH
        )

    x = x_ref[...].astype(jnp.float32).reshape(normed.shape)
    scale = lax.rsqrt(jnp.mean(x * x, axis=-1, keepdims=True) + EPSILON)
    normed[...] = (x * scale * gain_ref[...].astype(jnp.float32)).astype(jnp.bfloat16)

    for part in range(parts):

        @pl.loop(part * part_heads, (part + 1) * part_heads)
        def _(h):
            done = rotated(project(h, block_cols), q_gain_ref[...].astype(jnp.float32))
            done = [y.reshape(rows, steps, head_width) for y in done]
            at = pl.ds(pl.multiple_of(h * per_head, per_head), per_head)
            q_own[:, at, :] = jnp.concatenate(done, axis=1).astype(jnp.bfloat16)

        if part == 0:
            pl.semaphore_wait(barrier, n - 1)
        span = slice(part * part_rows, (part + 1) * part_rows)

        @pl.loop(1, n)
        def _(k):
            peer = after(k)
            for c in range(cap):
                q_send[part, peer, c] = q_own[own_row(peer, c), span]
            send_query(part, k).start()

        for c in range(cap):
            q_recv[part, me, c] = q_own[own_row(me, c), span]

    @pl.loop(0, key_blocks)
    def _(j):
        done = rotated(project(j + heads, key_cols), k_gain_ref[...].astype(jnp.float32))
        at = pl.ds(pl.multiple_of(j * key_cols, key_cols), key_cols)
        nk_ref[:, at] = jnp.concatenate(done, axis=1).astype(jnp.bfloat16)

    @pl.loop(0, key_blocks)
    def _(j):
        at = pl.ds(pl.multiple_of(j * key_cols, key_cols), key_cols)
        nv_ref[:, at] = project(j + heads + key_blocks, key_cols).astype(jnp.bfloat16)

    position = lax.broadcasted_iota(jnp.int32, (page, width), 0)

    def columns(h):
        return slice(h * head_width, (h + 1) * head_width)

    def stripe(h):
        return slice(h * per_head, (h + 1) * per_head)

    @pl.loop(0, n // PAIR)
    def _(turn):
        ks = [turn * PAIR + i for i in range(PAIR)]
        for k in ks:

            @pl.when(k + depth - PAIR < n)
            def _():
                for copy in fetch(k + depth - PAIR):
                    copy.start()

        for k in ks:

            @pl.when(k > 0)
            def _():
                for part in range(parts):
                    recv_query(part, k).wait_recv()

            for copy in fetch(k):
                copy.wait()

        slots = [(before(k), lax.rem(k, depth), c) for k in ks for c in range(cap)]
        scores = [
            spread_dot(
                kbuf[buf, c],
                jnp.concatenate([q_recv[part, owner, c] for part in range(parts)], axis=0),
                heads,
                per_head,
            )
            for owner, buf, c in slots
        ]
        turned = []
        for (owner, buf, c), found in zip(slots, scores):
            mask = position < usable_tokens(owner, c)
            top, total, weights = soft_parts(found, mask, head_width)
            s_send[owner, 2 * c : 2 * c + 1, 0:width] = top
            s_send[owner, 2 * c + 1 : 2 * c + 2, 0:width] = total
            turned.append(weights)
        for (owner, buf, c), weights in zip(slots, turned):
            for h in range(heads):
                o_send[owner, c, stripe(h)] = jnp.dot(
                    weights[stripe(h)],
                    vbuf[buf, c, :, columns(h)],
                    preferred_element_type=jnp.float32,
                ).astype(jnp.bfloat16)

        for k in ks:

            @pl.when(k > 0)
            def _():
                for copy in send_back(before(k), me):
                    copy.start()

    per_tile = 16 // steps
    token = lax.broadcasted_iota(jnp.int32, (16, width), 0)
    step = lax.rem(lax.broadcasted_iota(jnp.int32, (16, width), 1), steps)
    masks = [(token >= i * steps) & (token <= i * steps + step) for i in range(per_tile)]

    @pl.loop(0, rows // per_tile)
    def _(tile):
        at = pl.ds(pl.multiple_of(tile * 16, 16), 16)
        keys, values = nk_ref[at], nv_ref[at]
        scores = []
        for i in range(per_tile):
            scores.append(spread_dot(keys, q_own[tile * per_tile + i], heads, per_head))
        turned = []
        for i in range(per_tile):
            row = tile * per_tile + i
            top, total, weights = soft_parts(scores[i], masks[i], head_width)
            new_s[row, 0:1, 0:width] = top
            new_s[row, 1:2, 0:width] = total
            turned.append(weights)
        for h in range(heads):
            stacked = jnp.concatenate([w[stripe(h)] for w in turned], axis=0)
            outs = jnp.dot(stacked, values[:, columns(h)], preferred_element_type=jnp.float32)
            for i in range(per_tile):
                new_o[tile * per_tile + i, stripe(h)] = outs[stripe(i)]

    o_recv[me] = o_send[me]
    s_recv[me] = s_send[me]

    @pl.loop(1, n)
    def _(k):
        for part in range(parts):
            send_query(part, k).wait_send()
        for copy in send_back(before(k), me):
            copy.wait_send()
        for copy in send_back(after(k), after(k)):
            copy.wait_recv()

    @pl.loop(0, rows, unroll=2)
    def _(r):
        first, second = table_ref[3 * count + r], table_ref[3 * count + rows + r]
        has_second = table_ref[3 * count + 2 * rows + r]

        def stats(slot):
            both = s_recv[slot // cap]
            top, total = both[0:1], both[1:2]
            for c in range(1, cap):
                hit = lax.rem(slot, cap) == c
                top = jnp.where(hit, both[2 * c : 2 * c + 1], top)
                total = jnp.where(hit, both[2 * c + 1 : 2 * c + 2], total)
            return top, total

        top_a, total_a = stats(first)
        top_b, total_b = stats(second)
        top_b = jnp.where(has_second > 0, top_b, MASKED_SCORE)
        total_b = jnp.where(has_second > 0, total_b, 0.0)
        top_n, total_n = new_s[r, 0:1], new_s[r, 1:2]
        top = jnp.maximum(jnp.maximum(top_a, top_b), top_n)
        fa, fb, fn = jnp.exp(top_a - top), jnp.exp(top_b - top), jnp.exp(top_n - top)
        fb = jnp.where(has_second > 0, fb, 0.0)
        share = 1.0 / (fa * total_a + fb * total_b + fn * total_n)
        factors = jnp.concatenate(
            [fa * share, fb * share, fn * share, jnp.zeros((5, fa.shape[1]), jnp.float32)], axis=0
        ).T[0:width]
        out_a = o_recv[first // cap, lax.rem(first, cap)].astype(jnp.float32)
        out_b = o_recv[second // cap, lax.rem(second, cap)].astype(jnp.float32)
        out = factors[:, 0:1] * out_a + factors[:, 1:2] * out_b + factors[:, 2:3] * new_o[r]
        out_ref[r] = out.astype(out_ref.dtype)


def shards(
    hidden,
    norm_gain,
    w_query,
    key_projection,
    value_projection,
    query_gain,
    key_gain,
    cache_keys,
    cached_value_pages,
    cache_len,
    remaining,
    page_row,
    page_seq,
):
    gathered, full_gain = (
        lax.all_gather(hidden, "tp", axis=2, tiled=True),
        lax.all_gather(norm_gain, "tp", axis=0, tiled=True),
    )
    row_count, step_count, feature_count = gathered.shape
    head_width = query_gain.shape[0]
    groups = page_row.shape[0]
    capacity = page_row.shape[2]
    page_len = cache_keys.shape[3]
    kv_heads = key_projection.shape[1] // head_width
    my_group = lax.axis_index("dp")
    tokens = row_count * step_count
    local_lengths = lax.dynamic_slice_in_dim(cache_len, my_group * row_count, row_count)
    positions = local_lengths[:, None] + jnp.arange(step_count, dtype=jnp.int32)[None, :]
    half = head_width // 2
    frequency = jnp.exp(
        jnp.arange(half, dtype=jnp.float32) * (-2.0 * math.log(ROPE_BASE) / head_width)
    )
    angles = positions.astype(jnp.float32).reshape(tokens, 1) * frequency
    cosine, sine = jnp.cos(angles), jnp.sin(angles)
    cosine = jnp.concatenate([cosine, cosine], axis=1)
    sine = jnp.concatenate([-sine, sine], axis=1)
    query_heads = w_query.shape[1] // head_width
    group_size = query_heads // kv_heads
    per_head = group_size * step_count
    sent_rows = lax.dynamic_index_in_dim(page_row, my_group, 1, keepdims=False).reshape(-1)
    sent_seq = lax.dynamic_index_in_dim(page_seq, my_group, 1, keepdims=False).reshape(-1)
    row_index = jnp.arange(row_count, dtype=jnp.int32)[:, None]
    holds = sent_rows[None, :] == row_index
    slot_count = groups * capacity
    slot_index = jnp.arange(slot_count, dtype=jnp.int32)[None, :]
    shifted = slot_index * jnp.where(sent_seq == 0, 1, slot_count)[None, :]
    both = jnp.sum(jnp.where(holds, shifted, 0), axis=1)
    slot_a, slot_b = both % slot_count, both // slot_count
    has_b = (local_lengths > page_len).astype(jnp.int32)
    held_rows = lax.dynamic_index_in_dim(page_row, my_group, 0, keepdims=False).reshape(-1)
    held_seq = lax.dynamic_index_in_dim(page_seq, my_group, 0, keepdims=False).reshape(-1)
    table = jnp.concatenate(
        [jnp.minimum(sent_rows, row_count - 1), held_rows, held_seq, slot_a, slot_b, has_b]
    )
    width = kv_heads * per_head
    lanes = max(128, width)
    sizes = (row_count, kv_heads, per_head, head_width, step_count, capacity, page_len)
    parts = 2 if kv_heads % 2 == 0 else 1
    sizes = sizes + (DEPTH, parts)
    smem = pl.BlockSpec(memory_space=pltpu.SMEM)
    vmem = pl.BlockSpec(memory_space=pltpu.VMEM)
    hbm = pl.BlockSpec(memory_space=pl.ANY)
    bf16, f32 = jnp.bfloat16, jnp.float32
    features = kv_heads * head_width
    dma = pltpu.SemaphoreType.DMA
    attended, fresh_keys, fresh_values = pl.pallas_call(
        functools.partial(exchange_kernel, groups, sizes),
        out_shape=(
            jax.ShapeDtypeStruct((row_count, width, head_width), bf16),
            jax.ShapeDtypeStruct((tokens, features), bf16),
            jax.ShapeDtypeStruct((tokens, features), bf16),
        ),
        in_specs=[smem] * 2 + [vmem] * 6 + [hbm] * 5,
        out_specs=(vmem, vmem, vmem),
        scratch_shapes=[
            pltpu.VMEM((tokens, feature_count), bf16),
            pltpu.VMEM((WEIGHT_BUFFERS, feature_count, group_size * head_width), bf16),
            pltpu.VMEM((row_count, width, head_width), bf16),
            pltpu.VMEM((parts, groups, capacity, width // parts, head_width), bf16),
            pltpu.VMEM((parts, groups, capacity, width // parts, head_width), bf16),
            pltpu.VMEM((groups, capacity, width, head_width), bf16),
            pltpu.VMEM((groups, capacity, width, head_width), bf16),
            pltpu.VMEM((groups, 2 * capacity, lanes), f32),
            pltpu.VMEM((groups, 2 * capacity, lanes), f32),
            pltpu.VMEM((DEPTH, capacity, page_len, features), bf16),
            pltpu.VMEM((DEPTH, capacity, page_len, features), bf16),
            pltpu.VMEM((row_count, width, head_width), f32),
            pltpu.VMEM((row_count, 2, lanes), f32),
        ]
        + [dma((parts, groups))] * 2
        + [dma((groups,))] * 4
        + [dma((DEPTH,))] * 2
        + [dma((WEIGHT_BUFFERS,))],
        compiler_params=pltpu.CompilerParams(
            collective_id=0, has_side_effects=True, vmem_limit_bytes=56 * 1024 * 1024
        ),
        name="page_exchange",
    )(
        table,
        cache_len,
        gathered,
        full_gain.reshape(1, feature_count),
        cosine,
        sine,
        query_gain.reshape(1, head_width),
        key_gain.reshape(1, head_width),
        w_query,
        key_projection,
        value_projection,
        cache_keys.reshape(groups, capacity, page_len, features),
        cached_value_pages.reshape(groups, capacity, page_len, features),
    )
    attended = (
        attended.reshape(row_count, kv_heads, group_size, step_count, head_width)
        .transpose(0, 3, 1, 2, 4)
        .reshape(row_count, step_count, -1)
    )
    live = jnp.arange(step_count, dtype=jnp.int32)[None, :] < remaining[:, None]
    attention = jnp.where(live[:, :, None], attended, 0.0).astype(jnp.bfloat16)
    return (
        attention,
        fresh_keys.reshape(row_count, step_count, -1),
        fresh_values.reshape(row_count, step_count, -1),
    )


def solution(mesh):
    in_specs = (
        P("dp", None, "tp"),
        P("tp"),
        P(None, "tp"),
        P(None, "tp"),
        P(None, "tp"),
        P(),
        P(),
        P("dp", None, None, None, "tp"),
        P("dp", None, None, None, "tp"),
        P(),
        P("dp"),
        P(),
        P(),
    )
    out_specs = (P("dp", None, "tp"), P("dp", None, "tp"), P("dp", None, "tp"))
    return jax.shard_map(shards, mesh=mesh, in_specs=in_specs, out_specs=out_specs, check_vma=False)
```

```python
import functools
import math

import jax
import jax.numpy as jnp
from jax import lax
from jax.experimental import pallas as pl
from jax.experimental.pallas import tpu as pltpu
from jax.sharding import PartitionSpec as P

EPSILON = 1e-06
ROPE_BASE = 1000000.0
MASKED_SCORE = -1e30
DEPTH = 6
PAIR = 2
WEIGHT_BUFFERS = 3


def soft_parts(scores, mask, head_width):
    scores = jnp.where(mask, scores * (1.0 / math.sqrt(head_width)), MASKED_SCORE)
    top = jnp.maximum(jnp.max(scores, axis=0, keepdims=True), 0.1 * MASKED_SCORE)
    weights = jnp.exp(scores - top).astype(jnp.bfloat16).astype(jnp.float32)
    return top, jnp.sum(weights, axis=0, keepdims=True), weights.T.astype(jnp.bfloat16)


def spread_dot(keys, queries, heads, per_head):
    turned = queries.astype(jnp.float32).T.astype(jnp.bfloat16)
    head_of = lax.broadcasted_iota(jnp.int32, turned.shape, 1) // per_head
    spread = [jnp.where(head_of == h, turned, jnp.zeros_like(turned)) for h in range(heads)]
    return jnp.dot(
        keys, jnp.concatenate(spread, axis=0), preferred_element_type=jnp.float32
    )


def exchange_kernel(
    n,
    sizes,
    table_ref,
    len_ref,
    x_ref,
    gain_ref,
    cos_ref,
    sin_ref,
    q_gain_ref,
    k_gain_ref,
    wq_ref,
    wk_ref,
    wv_ref,
    ck_ref,
    cv_ref,
    out_ref,
    keys_ref,
    values_ref,
    normed,
    nk_ref,
    nv_ref,
    wbuf,
    q_own,
    q_send,
    q_recv,
    o_send,
    o_recv,
    s_send,
    s_recv,
    kbuf,
    vbuf,
    new_o,
    new_s,
    q_ssem,
    q_rsem,
    o_ssem,
    o_rsem,
    s_ssem,
    s_rsem,
    ksem,
    vsem,
    wsem,
):
    rows, heads, per_head, head_width, steps, cap, page, depth, parts = sizes
    width = heads * per_head
    part_heads = heads // parts
    group = 2 if heads % 2 == 0 else 1
    part_rows = part_heads * per_head
    block_cols = wbuf.shape[2]
    key_cols = min(block_cols, wk_ref.shape[1])
    key_blocks = wk_ref.shape[1] // key_cols
    blocks = heads + 2 * key_blocks
    bufs = wbuf.shape[0]
    me = lax.axis_index("dp")

    def distance(k):
        far_first = k // 2 + (n // 2) * lax.rem(k, 2)
        near_first = (k + 1) // 2 + (n // 2 - 1) * (1 - lax.rem(k, 2))
        ends = (k == 0) | (k == n - 1)
        return jnp.where((lax.rem(me, 2) == 0) | ends, far_first, near_first)

    def after(k):
        return lax.rem(me + distance(k), n)

    def before(k):
        return lax.rem(me + n - distance(k), n)

    count = n * cap

    def own_row(holder, c):
        return table_ref[holder * cap + c]

    def usable_tokens(owner, c):
        index = count + owner * cap + c
        row = table_ref[index]
        length = len_ref[owner * rows + jnp.minimum(row, rows - 1)]
        return jnp.where(row < rows, length, 0) - table_ref[index + count] * page

    def fetch(k):
        owner, buf = before(k), lax.rem(k, depth)
        return (
            pltpu.make_async_copy(ck_ref.at[owner], kbuf.at[buf], ksem.at[buf]),
            pltpu.make_async_copy(cv_ref.at[owner], vbuf.at[buf], vsem.at[buf]),
        )

    def weight(j, act):
        buf = lax.rem(j, bufs)

        def move(ref, at, cols):
            src = ref.at[:, pl.ds(pl.multiple_of(at * cols, cols), cols)]
            dst = wbuf.at[buf, :, pl.ds(0, cols)]
            act(pltpu.make_async_copy(src, dst, wsem.at[buf]))

        @pl.when(j < heads)
        def _():
            move(wq_ref, j, block_cols)

        @pl.when((j >= heads) & (j < heads + key_blocks))
        def _():
            move(wk_ref, j - heads, key_cols)

        @pl.when((j >= heads + key_blocks) & (j < blocks))
        def _():
            move(wv_ref, j - heads - key_blocks, key_cols)

    def start(copy):
        copy.start()

    def wait(copy):
        copy.wait()

    def project(j, cols):
        weight(j + bufs - 1, start)
        weight(j, wait)
        return jnp.dot(
            normed[...],
            wbuf[lax.rem(j, bufs), :, 0:cols],
            preferred_element_type=jnp.float32,
        )

    def rotated(made, gain):
        done = []
        for h in range(made.shape[1] // head_width):
            y = made[:, h * head_width : (h + 1) * head_width]
            y = y * lax.rsqrt(jnp.mean(y * y, axis=-1, keepdims=True) + EPSILON) * gain
            done.append(y * cos_ref[...] + pltpu.roll(y, head_width // 2, 1) * sin_ref[...])
        return done

    def send_query(part, k):
        peer = after(k)
        return pltpu.make_async_remote_copy(
            src_ref=q_send.at[part, peer],
            dst_ref=q_recv.at[part, me],
            send_sem=q_ssem.at[part, peer],
            recv_sem=q_rsem.at[part, me],
            device_id={"dp": peer},
            device_id_type=pl.DeviceIdType.MESH,
        )

    def recv_query(part, k):
        owner = before(k)
        return pltpu.make_async_remote_copy(
            src_ref=q_send.at[part, owner],
            dst_ref=q_recv.at[part, owner],
            send_sem=q_ssem.at[part, owner],
            recv_sem=q_rsem.at[part, owner],
            device_id={"dp": owner},
            device_id_type=pl.DeviceIdType.MESH,
        )

    def send_back(owner, slot):
        to = dict(device_id={"dp": owner}, device_id_type=pl.DeviceIdType.MESH)
        return (
            pltpu.make_async_remote_copy(
                src_ref=o_send.at[owner],
                dst_ref=o_recv.at[slot],
                send_sem=o_ssem.at[owner],
                recv_sem=o_rsem.at[slot],
                **to,
            ),
            pltpu.make_async_remote_copy(
                src_ref=s_send.at[owner],
                dst_ref=s_recv.at[slot],
                send_sem=s_ssem.at[owner],
                recv_sem=s_rsem.at[slot],
                **to,
            ),
        )

    for j in range(bufs - 1):
        weight(jnp.int32(j), start)
    for k in range(depth - PAIR):
        for copy in fetch(k):
            copy.start()

    barrier = pltpu.get_barrier_semaphore()

    @pl.loop(1, n)
    def _(k):
        pl.semaphore_signal(
            barrier, inc=1, device_id={"dp": after(k)}, device_id_type=pl.DeviceIdType.MESH
        )

    x = x_ref[...].astype(jnp.float32).reshape(normed.shape)
    scale = lax.rsqrt(jnp.mean(x * x, axis=-1, keepdims=True) + EPSILON)
    normed[...] = (x * scale * gain_ref[...].astype(jnp.float32)).astype(jnp.bfloat16)

    for part in range(parts):

        @pl.loop(part * part_heads, (part + 1) * part_heads)
        def _(h):
            done = rotated(project(h, block_cols), q_gain_ref[...].astype(jnp.float32))
            done = [y.reshape(rows, steps, head_width) for y in done]
            at = pl.ds(pl.multiple_of(h * per_head, per_head), per_head)
            q_own[:, at, :] = jnp.concatenate(done, axis=1).astype(jnp.bfloat16)

        if part == 0:
            pl.semaphore_wait(barrier, n - 1)
        span = slice(part * part_rows, (part + 1) * part_rows)

        @pl.loop(1, n)
        def _(k):
            peer = after(k)
            for c in range(cap):
                q_send[part, peer, c] = q_own[own_row(peer, c), span]
            send_query(part, k).start()

        for c in range(cap):
            q_recv[part, me, c] = q_own[own_row(me, c), span]

    @pl.loop(0, key_blocks)
    def _(j):
        done = rotated(project(j + heads, key_cols), k_gain_ref[...].astype(jnp.float32))
        at = pl.ds(pl.multiple_of(j * key_cols, key_cols), key_cols)
        made = jnp.concatenate(done, axis=1)
        nk_ref[:, at] = made.astype(jnp.bfloat16)
        keys_ref[:, :, at] = made.reshape(rows, steps, key_cols).astype(jnp.bfloat16)

    @pl.loop(0, key_blocks)
    def _(j):
        at = pl.ds(pl.multiple_of(j * key_cols, key_cols), key_cols)
        made = project(j + heads + key_blocks, key_cols)
        nv_ref[:, at] = made.astype(jnp.bfloat16)
        values_ref[:, :, at] = made.reshape(rows, steps, key_cols).astype(jnp.bfloat16)

    position = lax.broadcasted_iota(jnp.int32, (page, width), 0)

    def columns(h):
        return slice(h * head_width, (h + 1) * head_width)

    def stripe(h):
        return slice(h * per_head, (h + 1) * per_head)

    @pl.loop(0, n // PAIR)
    def _(turn):
        ks = [turn * PAIR + i for i in range(PAIR)]
        for k in ks:

            @pl.when(k + depth - PAIR < n)
            def _():
                for copy in fetch(k + depth - PAIR):
                    copy.start()

        for k in ks:

            @pl.when(k > 0)
            def _():
                for part in range(parts):
                    recv_query(part, k).wait_recv()

            for copy in fetch(k):
                copy.wait()

        slots = [(before(k), lax.rem(k, depth), c) for k in ks for c in range(cap)]
        scores = [
            spread_dot(
                kbuf[buf, c],
                jnp.concatenate([q_recv[part, owner, c] for part in range(parts)], axis=0),
                heads,
                per_head,
            )
            for owner, buf, c in slots
        ]
        turned = []
        for (owner, buf, c), found in zip(slots, scores):
            mask = position < usable_tokens(owner, c)
            top, total, weights = soft_parts(found, mask, head_width)
            s_send[owner, 2 * c : 2 * c + 1, 0:width] = top
            s_send[owner, 2 * c + 1 : 2 * c + 2, 0:width] = total
            turned.append(weights)
        for i in range(PAIR):
            owner, buf, _ = slots[i * cap]
            values = vbuf[buf].reshape(cap * page, heads * head_width)
            for h in range(0, heads, group):
                left = [
                    jnp.concatenate(
                        [
                            taken if c == other else jnp.zeros_like(taken)
                            for other in range(cap)
                        ],
                        axis=1,
                    )
                    for c, taken in enumerate(
                        turned[i * cap + c][h * per_head : (h + group) * per_head]
                        for c in range(cap)
                    )
                ]
                outs = jnp.dot(
                    jnp.concatenate(left, axis=0),
                    values[:, h * head_width : (h + group) * head_width],
                    preferred_element_type=jnp.float32,
                ).astype(jnp.bfloat16)
                for c in range(cap):
                    for j in range(group):
                        o_send[owner, c, stripe(h + j)] = outs[stripe(c * group + j), columns(j)]

        for k in ks:

            @pl.when(k > 0)
            def _():
                for copy in send_back(before(k), me):
                    copy.start()

    per_tile = 16 // steps
    token = lax.broadcasted_iota(jnp.int32, (16, width), 0)
    step = lax.rem(lax.broadcasted_iota(jnp.int32, (16, width), 1), steps)
    masks = [(token >= i * steps) & (token <= i * steps + step) for i in range(per_tile)]

    @pl.loop(0, rows // per_tile)
    def _(tile):
        at = pl.ds(pl.multiple_of(tile * 16, 16), 16)
        keys, values = nk_ref[at], nv_ref[at]
        scores = []
        for i in range(per_tile):
            scores.append(spread_dot(keys, q_own[tile * per_tile + i], heads, per_head))
        turned = []
        for i in range(per_tile):
            row = tile * per_tile + i
            top, total, weights = soft_parts(scores[i], masks[i], head_width)
            new_s[row, 0:1, 0:width] = top
            new_s[row, 1:2, 0:width] = total
            turned.append(weights)
        for h in range(heads):
            stacked = jnp.concatenate([w[stripe(h)] for w in turned], axis=0)
            outs = jnp.dot(stacked, values[:, columns(h)], preferred_element_type=jnp.float32)
            for i in range(per_tile):
                new_o[tile * per_tile + i, stripe(h)] = outs[stripe(i)]

    o_recv[me] = o_send[me]
    s_recv[me] = s_send[me]

    @pl.loop(1, n)
    def _(k):
        for part in range(parts):
            send_query(part, k).wait_send()
        for copy in send_back(before(k), me):
            copy.wait_send()
        for copy in send_back(after(k), after(k)):
            copy.wait_recv()

    def row_slots(r):
        at = 3 * count + r
        return table_ref[at], table_ref[at + rows], table_ref[at + 2 * rows]

    def stats(slot):
        both = s_recv[slot // cap]
        top, total = both[0:1], both[1:2]
        for c in range(1, cap):
            hit = lax.rem(slot, cap) == c
            top = jnp.where(hit, both[2 * c : 2 * c + 1], top)
            total = jnp.where(hit, both[2 * c + 1 : 2 * c + 2], total)
        return top, total

    shares = []
    for r in range(rows):
        first, second, has_second = row_slots(r)
        top_a, total_a = stats(first)
        top_b, total_b = stats(second)
        top_b = jnp.where(has_second > 0, top_b, MASKED_SCORE)
        top_n, total_n = new_s[r, 0:1], new_s[r, 1:2]
        top = jnp.maximum(jnp.maximum(top_a, top_b), top_n)
        fa, fb, fn = jnp.exp(top_a - top), jnp.exp(top_b - top), jnp.exp(top_n - top)
        fb = jnp.where(has_second > 0, fb, 0.0)
        share = 1.0 / (fa * total_a + fb * total_b + fn * total_n)
        shares += [fa * share, fb * share, fn * share]
    fill = -len(shares) % 128
    shares.append(jnp.zeros((fill, shares[0].shape[1]), jnp.float32))
    factors = jnp.concatenate(shares, axis=0).T[0:width]
    for r in range(rows):
        first, second, _ = row_slots(r)
        out_a = o_recv[first // cap, lax.rem(first, cap)].astype(jnp.float32)
        out_b = o_recv[second // cap, lax.rem(second, cap)].astype(jnp.float32)
        out = (
            factors[:, 3 * r : 3 * r + 1] * out_a
            + factors[:, 3 * r + 1 : 3 * r + 2] * out_b
            + factors[:, 3 * r + 2 : 3 * r + 3] * new_o[r]
        )
        out_ref[r] = out.astype(out_ref.dtype)


def shards(
    hidden,
    norm_gain,
    w_query,
    key_projection,
    value_projection,
    query_gain,
    key_gain,
    cache_keys,
    cached_value_pages,
    cache_len,
    remaining,
    page_row,
    page_seq,
):
    gathered, full_gain = (
        lax.all_gather(hidden, "tp", axis=2, tiled=True),
        lax.all_gather(norm_gain, "tp", axis=0, tiled=True),
    )
    row_count, step_count, feature_count = gathered.shape
    head_width = query_gain.shape[0]
    groups = page_row.shape[0]
    capacity = page_row.shape[2]
    page_len = cache_keys.shape[3]
    kv_heads = key_projection.shape[1] // head_width
    my_group = lax.axis_index("dp")
    tokens = row_count * step_count
    local_lengths = lax.dynamic_slice_in_dim(cache_len, my_group * row_count, row_count)
    positions = local_lengths[:, None] + jnp.arange(step_count, dtype=jnp.int32)[None, :]
    half = head_width // 2
    frequency = jnp.exp(
        jnp.arange(half, dtype=jnp.float32) * (-2.0 * math.log(ROPE_BASE) / head_width)
    )
    angles = positions.astype(jnp.float32).reshape(tokens, 1) * frequency
    cosine, sine = jnp.cos(angles), jnp.sin(angles)
    cosine = jnp.concatenate([cosine, cosine], axis=1)
    sine = jnp.concatenate([-sine, sine], axis=1)
    query_heads = w_query.shape[1] // head_width
    group_size = query_heads // kv_heads
    per_head = group_size * step_count
    sent_rows = lax.dynamic_index_in_dim(page_row, my_group, 1, keepdims=False).reshape(-1)
    sent_seq = lax.dynamic_index_in_dim(page_seq, my_group, 1, keepdims=False).reshape(-1)
    row_index = jnp.arange(row_count, dtype=jnp.int32)[:, None]
    holds = sent_rows[None, :] == row_index
    slot_count = groups * capacity
    slot_index = jnp.arange(slot_count, dtype=jnp.int32)[None, :]
    shifted = slot_index * jnp.where(sent_seq == 0, 1, slot_count)[None, :]
    both = jnp.sum(jnp.where(holds, shifted, 0), axis=1)
    slot_a, slot_b = both % slot_count, both // slot_count
    has_b = (local_lengths > page_len).astype(jnp.int32)
    held_rows = lax.dynamic_index_in_dim(page_row, my_group, 0, keepdims=False).reshape(-1)
    held_seq = lax.dynamic_index_in_dim(page_seq, my_group, 0, keepdims=False).reshape(-1)
    table = jnp.concatenate(
        [jnp.minimum(sent_rows, row_count - 1), held_rows, held_seq, slot_a, slot_b, has_b]
    )
    width = kv_heads * per_head
    lanes = max(128, width)
    sizes = (row_count, kv_heads, per_head, head_width, step_count, capacity, page_len)
    parts = math.gcd(4, kv_heads)
    sizes = sizes + (DEPTH, parts)
    smem = pl.BlockSpec(memory_space=pltpu.SMEM)
    vmem = pl.BlockSpec(memory_space=pltpu.VMEM)
    hbm = pl.BlockSpec(memory_space=pl.ANY)
    bf16, f32 = jnp.bfloat16, jnp.float32
    features = kv_heads * head_width
    dma = pltpu.SemaphoreType.DMA
    attended, fresh_keys, fresh_values = pl.pallas_call(
        functools.partial(exchange_kernel, groups, sizes),
        out_shape=(
            jax.ShapeDtypeStruct((row_count, width, head_width), bf16),
            jax.ShapeDtypeStruct((row_count, step_count, features), bf16),
            jax.ShapeDtypeStruct((row_count, step_count, features), bf16),
        ),
        in_specs=[smem] * 2 + [vmem] * 6 + [hbm] * 5,
        out_specs=(vmem, vmem, vmem),
        scratch_shapes=[
            pltpu.VMEM((tokens, feature_count), bf16),
            pltpu.VMEM((tokens, features), bf16),
            pltpu.VMEM((tokens, features), bf16),
            pltpu.VMEM((WEIGHT_BUFFERS, feature_count, group_size * head_width), bf16),
            pltpu.VMEM((row_count, width, head_width), bf16),
            pltpu.VMEM((parts, groups, capacity, width // parts, head_width), bf16),
            pltpu.VMEM((parts, groups, capacity, width // parts, head_width), bf16),
            pltpu.VMEM((groups, capacity, width, head_width), bf16),
            pltpu.VMEM((groups, capacity, width, head_width), bf16),
            pltpu.VMEM((groups, 2 * capacity, lanes), f32),
            pltpu.VMEM((groups, 2 * capacity, lanes), f32),
            pltpu.VMEM((DEPTH, capacity, page_len, features), bf16),
            pltpu.VMEM((DEPTH, capacity, page_len, features), bf16),
            pltpu.VMEM((row_count, width, head_width), f32),
            pltpu.VMEM((row_count, 2, lanes), f32),
        ]
        + [dma((parts, groups))] * 2
        + [dma((groups,))] * 4
        + [dma((DEPTH,))] * 2
        + [dma((WEIGHT_BUFFERS,))],
        compiler_params=pltpu.CompilerParams(
            collective_id=0, has_side_effects=True, vmem_limit_bytes=56 * 1024 * 1024
        ),
        name="page_exchange",
    )(
        table,
        cache_len,
        gathered,
        full_gain.reshape(1, feature_count),
        cosine,
        sine,
        query_gain.reshape(1, head_width),
        key_gain.reshape(1, head_width),
        w_query,
        key_projection,
        value_projection,
        cache_keys.reshape(groups, capacity, page_len, features),
        cached_value_pages.reshape(groups, capacity, page_len, features),
    )
    attended = (
        attended.reshape(row_count, kv_heads, group_size, step_count, head_width)
        .transpose(0, 3, 1, 2, 4)
        .reshape(row_count, step_count, -1)
    )
    live = jnp.arange(step_count, dtype=jnp.int32)[None, :] < remaining[:, None]
    attention = jnp.where(live[:, :, None], attended, 0.0).astype(jnp.bfloat16)
    return (
        attention,
        fresh_keys.reshape(row_count, step_count, -1),
        fresh_values.reshape(row_count, step_count, -1),
    )


def solution(mesh):
    in_specs = (
        P("dp", None, "tp"),
        P("tp"),
        P(None, "tp"),
        P(None, "tp"),
        P(None, "tp"),
        P(),
        P(),
        P("dp", None, None, None, "tp"),
        P("dp", None, None, None, "tp"),
        P(),
        P("dp"),
        P(),
        P(),
    )
    out_specs = (P("dp", None, "tp"), P("dp", None, "tp"), P("dp", None, "tp"))
    return jax.shard_map(shards, mesh=mesh, in_specs=in_specs, out_specs=out_specs, check_vma=False)
```
